512 devices in a mesh: ctx: 64 (over x, z, core), head: 8 (over y).
Axes of the slice: x: 4, y: 8, z: 8, core: 2. Of those that a mesh axis runs over, the one named last changes fastest.
Arguments:
- qkv: bfloat16 [1, 65536, 6144], P(None, ('ctx', 'head')), may hold values from -6 to 6
- grad_out: bfloat16 [1, 65536, 2048], P(None, ('ctx', 'head')), may hold values from -6 to 6
- w_qkv: bfloat16 [2048, 6144], P('ctx', 'head'), may hold values from -0.078125 to 0.078125
Outputs:
- grad_input: float32 [1, 65536, 2048], P(None, ('ctx', 'head'))
The draws below stay inside these ranges and needn't reach their ends.
All inputs are finite; a program needn't handle non-finite values.
Results may differ from the reference program's by a relative error of at most 0.02.
Values may be sent and summed in bfloat16 or wider, within the bound.
A program may use at most 128 MiB of HBM per device.

```python
import math
import jax
import jax.numpy as jnp
from jax import lax

D = 2048
HEADS = 16
DH = 128
BLOCK = 1024
SEQS = 1
HEADS_DEV = 2
LENGTH = 65536
N_CTX = 64
N_HEAD = 8


def levels(stream_key, shape, shards, smallest, top_value):
    loudness = 1.0
    for position, shards_of in shards:
        heights = jax.random.uniform(jax.random.fold_in(jax.random.fold_in(stream_key, 6), position), (shards_of,), jnp.float32, smallest / len(shards), top_value / len(shards))
        loudness = loudness * jnp.repeat(jnp.exp(heights), shape[position] // shards_of).reshape((-1,) + (1,) * (len(shape) - 1 - position))
    return loudness


def noise(stream_key, shape, width, bound, pieces=(), kind=jnp.bfloat16):
    array = width * jax.random.normal(stream_key, shape, jnp.float32)
    if pieces:
        array = array * levels(stream_key, shape, pieces, -0.22, 0.18)
    return jnp.clip(array, -bound, bound).astype(kind)


def setup_inputs(seed: int = 0) -> dict:
    seeds = jax.random.split(jax.random.key(seed), 4)
    qkv = noise(seeds[0], (SEQS, LENGTH, 3 * HEADS * DH), 1.0, 6.0, ((1, 512),))
    grad_out = noise(seeds[1], (SEQS, LENGTH, HEADS * DH), 1.0, 6.0, ((1, 512),))
    w_qkv = noise(seeds[2], (D, 3 * HEADS * DH), (3 * HEADS * DH) ** -0.5, 0.078125, ((0, 64), (1, 8)))
    return dict(qkv=qkv, grad_out=grad_out, w_qkv=w_qkv)


def attend(query_rows, key_rows, value_rows, grad_rows, causal):
    highest = lax.Precision.HIGHEST
    kv_own = jnp.einsum('sctd,scte->scde', key_rows, value_rows, precision=highest)
    qg_own = jnp.einsum('sctd,scte->scde', query_rows, grad_rows, precision=highest)
    kv_before = jnp.cumsum(kv_own, axis=1) - kv_own
    qg_after = lax.optimization_barrier(jnp.sum(qg_own, axis=1, keepdims=True)) - jnp.cumsum(qg_own, axis=1)
    scores_gv = jnp.einsum('scte,scue->sctu', grad_rows, value_rows, precision=highest) * causal
    scores_qk = jnp.einsum('sctd,scud->sctu', query_rows, key_rows, precision=highest) * causal
    grad_q = jnp.einsum('sctu,scud->sctd', scores_gv, key_rows, precision=highest) + jnp.einsum('scte,scde->sctd', grad_rows, kv_before, precision=highest)
    grad_k = jnp.einsum('sctu,sctd->scud', scores_gv, query_rows, precision=highest) + jnp.einsum('scue,scde->scud', value_rows, qg_after, precision=highest)
    grad_v = jnp.einsum('sctu,scte->scue', scores_qk, grad_rows, precision=highest) + jnp.einsum('scud,scde->scue', key_rows, qg_after, precision=highest)
    return jnp.stack([grad_q, grad_k, grad_v], axis=3)

def reference(qkv, grad_out, w_qkv):
    highest = lax.Precision.HIGHEST
    blocks = qkv.astype(jnp.float32).reshape(SEQS, N_CTX, BLOCK, HEADS, 3, DH)
    grads_in = grad_out.astype(jnp.float32).reshape(SEQS, N_CTX, BLOCK, HEADS, DH)
    causal = (jnp.arange(BLOCK)[:, None] >= jnp.arange(BLOCK)[None, :]).astype(jnp.float32)
    factor = 1.0 / math.sqrt(DH * LENGTH)

    def per_head(head_index):
        picked = lax.dynamic_index_in_dim(blocks, head_index, 3, keepdims=False)
        grad_rows = lax.dynamic_index_in_dim(grads_in, head_index, 3, keepdims=False)
        return attend(picked[:, :, :, 0], picked[:, :, :, 1], picked[:, :, :, 2], grad_rows, causal) * factor
    per_heads = lax.map(per_head, jnp.arange(HEADS, dtype=jnp.int32))
    gradients = jnp.transpose(per_heads, (1, 2, 3, 0, 4, 5)).astype(jnp.bfloat16).reshape(SEQS, LENGTH, HEADS * 3 * DH)
    group_width = HEADS_DEV * 3 * DH
    accum = jnp.zeros((SEQS, LENGTH, D), jnp.float32)
    for group in range(N_HEAD):
        start_col = group * group_width
        partial_sum = jnp.einsum('stf,df->std', gradients[:, :, start_col:start_col + group_width].astype(jnp.float32), w_qkv[:, start_col:start_col + group_width].astype(jnp.float32), precision=highest)
        rounded = lax.optimization_barrier(partial_sum.astype(jnp.bfloat16))
        accum = accum + rounded.astype(jnp.float32)
    return accum
```

```python
import functools
import math

import jax
import jax.numpy as jnp
from jax import lax
from jax.experimental import pallas as pl
from jax.experimental.pallas import tpu as pltpu
from jax.sharding import PartitionSpec as P

DH = 128
W3 = 3 * DH
MESH = pl.DeviceIdType.MESH
NX, NY, NZ = 4, 8, 8
F32, BF16 = jnp.float32, jnp.bfloat16


def where_am_i():
    ctx, y = lax.axis_index("ctx"), lax.axis_index("head")
    c, xz = lax.rem(ctx, 2), lax.div(ctx, 2)
    return lax.div(xz, NZ), y, lax.rem(xz, NZ), c


def device(x, y, z, c):
    return ((x * NZ + z) * 2 + c, y)


def nn(a, b):
    return lax.dot_general(a, b, (((1,), (0,)), ((), ())), preferred_element_type=F32)


def nt(a, b):
    return lax.dot_general(a, b, (((1,), (1,)), ((), ())), preferred_element_type=F32)


def tn(a, b):
    return lax.dot_general(a, b, (((0,), (0,)), ((), ())), preferred_element_type=F32)


def lanes(index, width):
    return pl.ds(pl.multiple_of(index * width, width), width)


def attention_kernel(
    factor, qkv_ref, grad_ref, out_ref,
    got_qkv, got_grad, states, arrived, before, intra, total, z_in, x_in, z_out, base,
    core_sem, state_send, state_recv, z_send, z_recv, x_send, x_recv, b_send, b_recv, p_send, p_recv,
):
    x, y, z, c = where_am_i()
    other = 1 - c
    ring_y = lambda k: device(x, lax.rem(y + k, NY), z, c)
    ring_z = lambda k: device(x, y, lax.rem(z + k, NZ), c)
    ring_x = lambda k: device(lax.rem(x + k, NX), y, z, c)
    partner = device(x, y, z, other)

    barrier = pltpu.get_barrier_semaphore()
    everyone = [partner] + [ring_y(k) for k in range(1, NY)]
    everyone += [ring_z(k) for k in range(1, NZ)] + [ring_x(k) for k in range(1, NX)]
    for peer in everyone:
        pl.semaphore_signal(barrier, inc=1, device_id=peer, device_id_type=MESH)
    pl.semaphore_wait(barrier, len(everyone))

    def swap(j):
        send = pltpu.make_async_remote_copy(
            qkv_ref.at[:, lanes(2 * j + other, W3)], got_qkv.at[:, lanes(j, W3)],
            core_sem.at[0, j], core_sem.at[1, j], device_id=partner, device_id_type=MESH)
        send_grad = pltpu.make_async_remote_copy(
            grad_ref.at[:, lanes(2 * j + other, DH)], got_grad.at[:, lanes(j, DH)],
            core_sem.at[2, j], core_sem.at[3, j], device_id=partner, device_id_type=MESH)
        return send, send_grad

    def y_of(k):
        return lax.rem(y + k, NY)

    def start_swap(k, carry):
        for copy in swap(y_of(k)):
            copy.start()
        return carry

    lax.fori_loop(0, NY, start_swap, 0)

    def own_rows(j):
        at = (2 * j + c) * W3
        part = lambda i: qkv_ref[:, pl.ds(pl.multiple_of(at + i * DH, DH), DH)]
        return part(0), part(1), part(2), grad_ref[:, lanes(2 * j + c, DH)]

    def got_rows(j):
        part = lambda i: got_qkv[:, pl.ds(pl.multiple_of(j * W3 + i * DH, DH), DH)]
        return part(0), part(1), part(2), got_grad[:, lanes(j, DH)]

    def state_copy(k):
        return pltpu.make_async_remote_copy(
            states.at[y_of(k)], arrived.at[y], state_send.at[k], state_recv.at[k],
            device_id=ring_y(k), device_id_type=MESH)

    def block_states(into, j):
        for slot, rows in ((c, own_rows(j)), (other, got_rows(j))):
            q, k, v, g = rows
            into[j, slot, 0] = tn(k, v).astype(BF16)
            into[j, slot, 1] = tn(q, g).astype(BF16)

    def make_states(k, carry):
        j = y_of(k)
        for copy in swap(j):
            copy.wait()
        block_states(states, j)
        state_copy(k).start()
        return carry

    lax.fori_loop(1, NY, make_states, 0)
    for copy in swap(y):
        copy.wait()
    block_states(arrived, y)

    rows_at = lax.broadcasted_iota(jnp.int32, (DH, DH), 0)
    cols_at = lax.broadcasted_iota(jnp.int32, (DH, DH), 1)
    causal = rows_at >= cols_at

    def inside(j, carry):
        for slot, rows in ((c, own_rows(j)), (other, got_rows(j))):
            q, k, v, g = rows
            gv = jnp.where(causal, nt(g, v), 0.0).astype(BF16)
            qk = jnp.where(causal, nt(q, k), 0.0).astype(BF16)
            intra[slot, j, 0] = nn(gv, k)
            intra[slot, j, 1] = tn(gv, q)
            intra[slot, j, 2] = tn(qk, g)
        return carry

    lax.fori_loop(0, NY, inside, 0)

    def wait_state(k, carry):
        state_copy(k).wait()
        return carry

    lax.fori_loop(1, NY, wait_state, 0)

    for kind in range(2):
        acc = jnp.zeros((DH, DH), F32)
        for j in range(NY):
            acc = acc + arrived[j, 0, kind].astype(F32) + arrived[j, 1, kind].astype(F32)
        total[pl.ds(kind * DH, DH), :] = acc
    part = 2 * DH // NZ

    def slice_of(i):
        return pl.ds(pl.multiple_of(i * part, part), part)

    def z_copy(k):
        return pltpu.make_async_remote_copy(
            total.at[slice_of(lax.rem(z + k, NZ))], z_in.at[z], z_send.at[k], z_recv.at[k],
            device_id=ring_z(k), device_id_type=MESH)

    for k in range(1, NZ):
        z_copy(k).start()
    z_in[z] = total[slice_of(z), :]
    for k in range(1, NZ):
        z_copy(k).wait()
    sums = [jnp.zeros((part, DH), F32)]
    for i in range(NZ):
        sums.append(sums[-1] + z_in[i])
    x_in[x] = sums[NZ]

    def x_copy(k):
        return pltpu.make_async_remote_copy(
            x_in.at[x], x_in.at[x], x_send.at[k], x_recv.at[k],
            device_id=ring_x(k), device_id_type=MESH)

    for k in range(1, NX):
        x_copy(k).start()
    forward = z < NZ // 2
    for k in range(1, NX):
        x_copy(k).wait()
    far = jnp.zeros((part, DH), F32)
    for i in range(NX):
        counts = jnp.where(forward, i < x, i > x)
        far = far + jnp.where(counts, x_in[i], 0.0)
    for i in range(NZ):
        near = jnp.where(forward, sums[i], sums[NZ] - sums[i + 1])
        z_out[i] = far + near

    def b_copy(k):
        return pltpu.make_async_remote_copy(
            z_out.at[lax.rem(z + k, NZ)], base.at[slice_of(z)], b_send.at[k], b_recv.at[k],
            device_id=ring_z(k), device_id_type=MESH)

    for k in range(1, NZ):
        b_copy(k).start()
    base[slice_of(z), :] = z_out[z]
    for k in range(1, NZ):
        b_copy(k).wait()

    acc = base[pl.ds(0, DH), :]
    for slot in range(2):
        for j in range(NY):
            states[j, slot, 0] = acc.astype(BF16)
            acc = acc + arrived[j, slot, 0].astype(F32)
    acc = base[pl.ds(DH, DH), :]
    for slot in (1, 0):
        for j in reversed(range(NY)):
            states[j, slot, 1] = acc.astype(BF16)
            acc = acc + arrived[j, slot, 1].astype(F32)

    def p_copy(k):
        return pltpu.make_async_remote_copy(
            states.at[y_of(k)], before.at[y], p_send.at[k], p_recv.at[k],
            device_id=ring_y(k), device_id_type=MESH)

    def start_p(k, carry):
        p_copy(k).start()
        return carry

    lax.fori_loop(1, NY, start_p, 0)
    for slot in range(2):
        for kind in range(2):
            before[y, slot, kind] = states[y, slot, kind]

    def finish(j):
        for slot, rows in ((c, own_rows(j)), (other, got_rows(j))):
            q, k, v, g = rows
            kv, qg = before[j, slot, 0], before[j, slot, 1]
            at = lambda i: pl.ds(pl.multiple_of(j * W3 + i * DH, DH), DH)
            out_ref[slot, :, at(0)] = ((intra[slot, j, 0] + nt(g, kv)) * factor).astype(BF16)
            out_ref[slot, :, at(1)] = ((intra[slot, j, 1] + nt(v, qg)) * factor).astype(BF16)
            out_ref[slot, :, at(2)] = ((intra[slot, j, 2] + nn(k, qg)) * factor).astype(BF16)

    finish(y)

    def finish_got(k, carry):
        p_copy(k).wait()
        finish(lax.rem(y - k + NY, NY))
        return carry

    lax.fori_loop(1, NY, finish_got, 0)


def attention(qkv, grad, factor):
    state = pltpu.VMEM((NY, 2, 2, DH, DH), BF16)
    part = 2 * DH // NZ
    pairs = [pltpu.SemaphoreType.DMA((n,)) for n in (NY, NY, NZ, NZ, NX, NX, NZ, NZ, NY, NY)]
    return pl.pallas_call(
        functools.partial(attention_kernel, factor),
        out_shape=jax.ShapeDtypeStruct((2, DH, NY * W3), BF16),
        in_specs=[pl.BlockSpec(memory_space=pltpu.VMEM)] * 2,
        out_specs=pl.BlockSpec(memory_space=pltpu.VMEM),
        scratch_shapes=[
            pltpu.VMEM((DH, NY * W3), BF16), pltpu.VMEM((DH, NY * DH), BF16),
            state, state, state,
            pltpu.VMEM((2, NY, 3, DH, DH), F32),
            pltpu.VMEM((2 * DH, DH), F32), pltpu.VMEM((NZ, part, DH), F32),
            pltpu.VMEM((NX, part, DH), F32), pltpu.VMEM((NZ, part, DH), F32),
            pltpu.VMEM((2 * DH, DH), F32),
            pltpu.SemaphoreType.DMA((4, NY)), *pairs,
        ],
        compiler_params=pltpu.CompilerParams(
            collective_id=0, has_side_effects=True, vmem_limit_bytes=24 << 20),
        cost_estimate=pl.CostEstimate(flops=2 * 10**9, bytes_accessed=200 * 10**6, transcendentals=0),
        name="attention",
    )(qkv, grad)


def per_device(qkv, grad_out, w_qkv):
    n = lax.axis_size("ctx")
    factor = 1.0 / math.sqrt(DH * DH * NY * n)
    c = lax.rem(lax.axis_index("ctx"), 2)
    halves = jnp.stack([w_qkv[:, :W3], w_qkv[:, W3:]])
    keep = lax.dynamic_index_in_dim(halves, c, 0, False)
    give = lax.dynamic_index_in_dim(halves, 1 - c, 0, False)
    got = lax.ppermute(give, "ctx", [(i, i ^ 1) for i in range(n)])
    pair = jnp.where(c == 0, jnp.stack([keep, got]), jnp.stack([got, keep]))
    groups = [[2 * i + core for i in range(n // 2)] for core in range(2)]
    by_head = lax.all_gather(pair, "head")
    whole = lax.all_gather(by_head, "ctx", axis_index_groups=groups)
    grads = attention(qkv[0], grad_out[0], factor)
    grads = grads.reshape(2, DH, NY, W3)
    partial = jnp.einsum("btyf,xyprf->btxpr", grads, whole, preferred_element_type=F32)
    partial = partial.reshape(2, DH, -1)
    mine = lax.dynamic_index_in_dim(partial, c, 0, False)
    theirs = lax.dynamic_index_in_dim(partial, 1 - c, 0, False).astype(BF16)
    other = lax.ppermute(theirs, "ctx", [(i, i ^ 1) for i in range(n)])
    return (mine + other.astype(F32))[None]


def solution(mesh):
    spec = P(None, ("ctx", "head"), None)
    return jax.shard_map(
        per_device, mesh=mesh, in_specs=(spec, spec, P("ctx", "head")), out_specs=spec, check_vma=False)
```

```python
import functools
import math

import jax
import jax.numpy as jnp
from jax import lax
from jax.experimental import pallas as pl
from jax.experimental.pallas import tpu as pltpu
from jax.sharding import PartitionSpec as P

DH = 128
W3 = 3 * DH
MESH = pl.DeviceIdType.MESH
NX, NY, NZ = 4, 8, 8
F32, BF16 = jnp.float32, jnp.bfloat16
TILE = 256
PLAN = [
    [("a", 0), ("b", 0)],
    [],
    [],
    [("a", 1)],
    [("a", 2), ("b", 1)],
    [("a", 3), ("b", 2)],
    [("a", 4), ("b", 3), ("a", 5), ("b", 4), ("a", 6)],
    [("a", 7), ("b", 5), ("a", 8), ("b", 6)],
]


def where_am_i():
    ctx, y = lax.axis_index("ctx"), lax.axis_index("head")
    c, xz = lax.rem(ctx, 2), lax.div(ctx, 2)
    return lax.div(xz, NZ), y, lax.rem(xz, NZ), c


def device(x, y, z, c):
    return ((x * NZ + z) * 2 + c, y)


def nn(a, b):
    return lax.dot_general(a, b, (((1,), (0,)), ((), ())), preferred_element_type=F32)


def nt(a, b):
    return lax.dot_general(a, b, (((1,), (1,)), ((), ())), preferred_element_type=F32)


def tn(a, b):
    return lax.dot_general(a, b, (((0,), (0,)), ((), ())), preferred_element_type=F32)


def lanes(index, width):
    return pl.ds(pl.multiple_of(index * width, width), width)


def layer_kernel(
    factor, qkv_ref, grad_ref, w_ref, out_ref,
    got_qkv, got_grad, states, arrived, before, intra, total, z_in, x_in, z_out, base, grads, weight, give, take,
    core_sem, state_send, state_recv, z_send, z_recv, x_send, x_recv, b_send, b_recv, p_send, p_recv,
    w_sem, first_sem, ring_sem, line_sem, cross_sem, long_sem, tile_sem,
):
    x, y, z, c = where_am_i()
    other = 1 - c
    ring_y = lambda k: device(x, lax.rem(y + k, NY), z, c)
    ring_z = lambda k: device(x, y, lax.rem(z + k, NZ), c)
    ring_x = lambda k: device(lax.rem(x + k, NX), y, z, c)
    partner = device(x, y, z, other)

    barrier = pltpu.get_barrier_semaphore()
    everyone = [partner] + [ring_y(k) for k in range(1, NY)]
    everyone += [ring_z(k) for k in range(1, NZ)] + [ring_x(k) for k in range(1, NX)]
    for peer in everyone:
        pl.semaphore_signal(barrier, inc=1, device_id=peer, device_id_type=MESH)
    pl.semaphore_wait(barrier, len(everyone))

    spot = x * NZ + z
    rows = w_ref.shape[0]
    half = rows // 2

    def send(ref, sems, at, peer):
        return pltpu.make_async_remote_copy(
            ref, ref, sems.at[(0,) + at], sems.at[(1,) + at], device_id=peer, device_id_type=MESH)

    own_half = pl.ds(pl.multiple_of(c * rows, rows), rows)
    swap_w = pltpu.make_async_remote_copy(
        w_ref.at[:, lanes(other, W3)], weight.at[y, spot, own_half],
        w_sem.at[0], w_sem.at[1], device_id=partner, device_id_type=MESH)
    swap_w.start()

    def side(way, last):
        return pl.ds(0 if way > 0 else half, half) if last else pl.ds(0, rows)

    def side_z(way, last):
        return pl.ds(rows if way > 0 else rows + half, half) if last else pl.ds(rows, rows)

    def way_at(way):
        return 0 if way > 0 else 1

    def a_first(k):
        return send(weight.at[y, spot, pl.ds(0, rows)], first_sem, (0, k), ring_z(k))

    def b_first(k):
        return send(weight.at[y, spot, pl.ds(rows, rows)], first_sem, (1, k), ring_y(k))

    def a_ring(way, d):
        block = weight.at[lax.rem(y - way * d + NY, NY), pl.ds(x * NZ, NZ), side(way, d == NY // 2 - 1)]
        return send(block, ring_sem, (way_at(way), d), ring_y(way % NY))

    order = [0, -1, 1, -2, 2, -3, 3, 4]

    def a_line(t, way, d):
        at = lax.rem(x - way * d + NX, NX)
        block = weight.at[lax.rem(y + order[t] + NY, NY), pl.ds(at * NZ, NZ), side(way, d == 1)]
        return send(block, line_sem, (t, way_at(way), d), ring_x(way % NX))

    def b_cross(way, d):
        at = lax.rem(x - way * d + NX, NX)
        return send(weight.at[:, at * NZ + z, side_z(way, d == 1)], cross_sem, (way_at(way), d), ring_x(way % NX))

    def b_long(b, way, d):
        at = lax.rem(x + (0, -1, 1, 2)[b] + NX, NX) * NZ + lax.rem(z - way * d + NZ, NZ)
        block = weight.at[:, at, side_z(way, d == NZ // 2 - 1)]
        return send(block, long_sem, (b, way_at(way), d), ring_z(way % NZ))

    both = (1, -1)

    def step_a(t):
        if t == 0:
            for way in both:
                a_ring(way, 0).start()
        elif t < NY - 1:
            way, d = both[(t - 1) % 2], (t - 1) // 2
            a_ring(way, d).wait_recv()
            a_ring(way, d + 1).start()
        elif t == NY - 1:
            for way in both:
                a_ring(way, NY // 2 - 1).wait_recv()
        if t < NY:
            for way in both:
                a_line(t, way, 0).start()
        if t >= 1:
            for way in both:
                a_line(t - 1, way, 0).wait_recv()
                a_line(t - 1, way, 1).start()

    def step_b(s):
        if s == 0:
            for way in both:
                b_cross(way, 0).start()
        elif s == 1:
            for way in both:
                b_cross(way, 0).wait_recv()
                b_cross(way, 1).start()
        elif s == 3:
            for way in both:
                b_cross(way, 1).wait_recv()
        if s < NX:
            for way in both:
                b_long(s, way, 0).start()
        for d in range(NZ // 2 - 1):
            b = s - 1 - d
            if 0 <= b < NX:
                for way in both:
                    b_long(b, way, d).wait_recv()
                    b_long(b, way, d + 1).start()

    def finish_weight():
        for way in both:
            for t in range(NY):
                a_line(t, way, 1).wait_recv()
                a_line(t, way, 0).wait_send()
                a_line(t, way, 1).wait_send()
            for d in range(NY // 2):
                a_ring(way, d).wait_send()
            for d in range(2):
                b_cross(way, d).wait_send()
            for b in range(NX):
                b_long(b, way, NZ // 2 - 1).wait_recv()
                for d in range(NZ // 2):
                    b_long(b, way, d).wait_send()

    def swap(j):
        send = pltpu.make_async_remote_copy(
            qkv_ref.at[:, lanes(2 * j + other, W3)], got_qkv.at[:, lanes(j, W3)],
            core_sem.at[0, j], core_sem.at[1, j], device_id=partner, device_id_type=MESH)
        send_grad = pltpu.make_async_remote_copy(
            grad_ref.at[:, lanes(2 * j + other, DH)], got_grad.at[:, lanes(j, DH)],
            core_sem.at[2, j], core_sem.at[3, j], device_id=partner, device_id_type=MESH)
        return send, send_grad

    def y_of(k):
        return lax.rem(y + k, NY)

    def start_swap(k, carry):
        for copy in swap(y_of(k)):
            copy.start()
        return carry

    lax.fori_loop(0, NY, start_swap, 0)

    weight[y, spot, own_half, :] = w_ref[:, lanes(c, W3)]
    swap_w.wait()

    def start_first(k, carry):
        a_first(k).start()
        b_first(k).start()
        return carry

    lax.fori_loop(1, NY, start_first, 0)

    def wait_a_first(k, carry):
        a_first(k).wait()
        return carry

    def wait_b_first(k, carry):
        b_first(k).wait()
        return carry

    def run(steps):
        for name, number in steps:
            if name == "a":
                if number == 0:
                    lax.fori_loop(1, NZ, wait_a_first, 0)
                step_a(number)
            else:
                if number == 0:
                    lax.fori_loop(1, NY, wait_b_first, 0)
                step_b(number)

    def own_rows(j):
        at = (2 * j + c) * W3
        part = lambda i: qkv_ref[:, pl.ds(pl.multiple_of(at + i * DH, DH), DH)]
        return part(0), part(1), part(2), grad_ref[:, lanes(2 * j + c, DH)]

    def got_rows(j):
        part = lambda i: got_qkv[:, pl.ds(pl.multiple_of(j * W3 + i * DH, DH), DH)]
        return part(0), part(1), part(2), got_grad[:, lanes(j, DH)]

    def state_copy(k):
        return pltpu.make_async_remote_copy(
            states.at[y_of(k)], arrived.at[y], state_send.at[k], state_recv.at[k],
            device_id=ring_y(k), device_id_type=MESH)

    def block_states(into, j):
        for slot, rows in ((c, own_rows(j)), (other, got_rows(j))):
            q, k, v, g = rows
            into[j, slot, 0] = tn(k, v).astype(BF16)
            into[j, slot, 1] = tn(q, g).astype(BF16)

    def make_states(k, carry):
        j = y_of(k)
        for copy in swap(j):
            copy.wait()
        block_states(states, j)
        state_copy(k).start()
        return carry

    lax.fori_loop(1, 5, make_states, 0)
    run(PLAN[0])
    lax.fori_loop(5, NY, make_states, 0)
    for copy in swap(y):
        copy.wait()
    block_states(arrived, y)
    run(PLAN[1])

    rows_at = lax.broadcasted_iota(jnp.int32, (DH, DH), 0)
    cols_at = lax.broadcasted_iota(jnp.int32, (DH, DH), 1)
    causal = rows_at >= cols_at

    def inside(j, carry):
        for slot, rows in ((c, own_rows(j)), (other, got_rows(j))):
            q, k, v, g = rows
            gv = jnp.where(causal, nt(g, v), 0.0).astype(BF16)
            qk = jnp.where(causal, nt(q, k), 0.0).astype(BF16)
            intra[slot, j, 0] = nn(gv, k)
            intra[slot, j, 1] = tn(gv, q)
            intra[slot, j, 2] = tn(qk, g)
        return carry

    for piece in range(4):
        lax.fori_loop(2 * piece, 2 * piece + 2, inside, 0)
        run(PLAN[2 + piece])

    def wait_state(k, carry):
        state_copy(k).wait()
        return carry

    lax.fori_loop(1, NY, wait_state, 0)

    for kind in range(2):
        acc = jnp.zeros((DH, DH), F32)
        for j in range(NY):
            acc = acc + arrived[j, 0, kind].astype(F32) + arrived[j, 1, kind].astype(F32)
        total[pl.ds(kind * DH, DH), :] = acc
    part = 2 * DH // NZ

    def slice_of(i):
        return pl.ds(pl.multiple_of(i * part, part), part)

    def z_copy(k):
        return pltpu.make_async_remote_copy(
            total.at[slice_of(lax.rem(z + k, NZ))], z_in.at[z], z_send.at[k], z_recv.at[k],
            device_id=ring_z(k), device_id_type=MESH)

    for k in range(1, NZ):
        z_copy(k).start()
    z_in[z] = total[slice_of(z), :]
    for k in range(1, NZ):
        z_copy(k).wait()
    sums = [jnp.zeros((part, DH), F32)]
    for i in range(NZ):
        sums.append(sums[-1] + z_in[i])
    x_in[x] = sums[NZ]

    def x_copy(k):
        return pltpu.make_async_remote_copy(
            x_in.at[x], x_in.at[x], x_send.at[k], x_recv.at[k],
            device_id=ring_x(k), device_id_type=MESH)

    for k in range(1, NX):
        x_copy(k).start()
    forward = z < NZ // 2
    for k in range(1, NX):
        x_copy(k).wait()
    far = jnp.zeros((part, DH), F32)
    for i in range(NX):
        counts = jnp.where(forward, i < x, i > x)
        far = far + jnp.where(counts, x_in[i], 0.0)
    for i in range(NZ):
        near = jnp.where(forward, sums[i], sums[NZ] - sums[i + 1])
        z_out[i] = far + near

    def b_copy(k):
        return pltpu.make_async_remote_copy(
            z_out.at[lax.rem(z + k, NZ)], base.at[slice_of(z)], b_send.at[k], b_recv.at[k],
            device_id=ring_z(k), device_id_type=MESH)

    for k in range(1, NZ):
        b_copy(k).start()
    base[slice_of(z), :] = z_out[z]
    for k in range(1, NZ):
        b_copy(k).wait()

    acc = base[pl.ds(0, DH), :]
    for slot in range(2):
        for j in range(NY):
            states[j, slot, 0] = acc.astype(BF16)
            acc = acc + arrived[j, slot, 0].astype(F32)
    acc = base[pl.ds(DH, DH), :]
    for slot in (1, 0):
        for j in reversed(range(NY)):
            states[j, slot, 1] = acc.astype(BF16)
            acc = acc + arrived[j, slot, 1].astype(F32)

    def p_copy(k):
        return pltpu.make_async_remote_copy(
            states.at[y_of(k)], before.at[y], p_send.at[k], p_recv.at[k],
            device_id=ring_y(k), device_id_type=MESH)

    def start_p(k, carry):
        p_copy(k).start()
        return carry

    lax.fori_loop(1, NY, start_p, 0)
    run(PLAN[6])
    for slot in range(2):
        for kind in range(2):
            before[y, slot, kind] = states[y, slot, kind]

    def finish(j):
        for slot, mine, rows_of in ((c, 0, own_rows), (other, 1, got_rows)):
            q, k, v, g = rows_of(j)
            kv, qg = before[j, slot, 0], before[j, slot, 1]
            at = lambda i: pl.ds(pl.multiple_of(j * W3 + i * DH, DH), DH)
            grads[mine, :, at(0)] = ((intra[slot, j, 0] + nt(g, kv)) * factor).astype(BF16)
            grads[mine, :, at(1)] = ((intra[slot, j, 1] + nt(v, qg)) * factor).astype(BF16)
            grads[mine, :, at(2)] = ((intra[slot, j, 2] + nn(k, qg)) * factor).astype(BF16)

    finish(y)

    def finish_got(k, carry):
        p_copy(k).wait()
        finish(lax.rem(y - k + NY, NY))
        return carry

    lax.fori_loop(1, NY, finish_got, 0)
    run(PLAN[7])
    finish_weight()

    tiles = NX * NZ * 2 * rows // TILE
    spots = TILE // (2 * rows)

    def tile_copy(i):
        return pltpu.make_async_remote_copy(
            give.at[:, lanes(i, TILE)], take.at[:, lanes(i, TILE)],
            tile_sem.at[0, i], tile_sem.at[1, i], device_id=partner, device_id_type=MESH)

    def project(i, carry):
        acc = jnp.zeros((2 * DH, TILE), F32)
        for j in range(NY):
            left = grads[:, :, j * W3:(j + 1) * W3].reshape(2 * DH, W3)
            right = weight[j, pl.ds(i * spots, spots)].reshape(TILE, W3)
            acc = acc + nt(left, right)
        give[:, lanes(i, TILE)] = acc[DH:].astype(BF16)
        tile_copy(i).start()
        out_ref[:, lanes(i, TILE)] = acc[:DH]
        return carry

    lax.fori_loop(0, tiles, project, 0)

    def add_partner(i, carry):
        tile_copy(i).wait()
        out_ref[:, lanes(i, TILE)] += take[:, lanes(i, TILE)].astype(F32)
        return carry

    lax.fori_loop(0, tiles, add_partner, 0)


def layer(qkv, grad, w, factor):
    state = pltpu.VMEM((NY, 2, 2, DH, DH), BF16)
    part = 2 * DH // NZ
    rows = w.shape[0]
    width = NX * NZ * 2 * rows
    dma = pltpu.SemaphoreType.DMA
    pairs = [dma((n,)) for n in (NY, NY, NZ, NZ, NX, NX, NZ, NZ, NY, NY)]
    vmem = pl.BlockSpec(memory_space=pltpu.VMEM)
    return pl.pallas_call(
        functools.partial(layer_kernel, factor),
        out_shape=jax.ShapeDtypeStruct((DH, width), F32),
        in_specs=[vmem] * 3,
        out_specs=vmem,
        scratch_shapes=[
            pltpu.VMEM((DH, NY * W3), BF16), pltpu.VMEM((DH, NY * DH), BF16),
            state, state, state,
            pltpu.VMEM((2, NY, 3, DH, DH), F32),
            pltpu.VMEM((2 * DH, DH), F32), pltpu.VMEM((NZ, part, DH), F32),
            pltpu.VMEM((NX, part, DH), F32), pltpu.VMEM((NZ, part, DH), F32),
            pltpu.VMEM((2 * DH, DH), F32),
            pltpu.VMEM((2, DH, NY * W3), BF16),
            pltpu.VMEM((NY, NX * NZ, 2 * rows, W3), BF16),
            pltpu.VMEM((DH, width), BF16), pltpu.VMEM((DH, width), BF16),
            dma((4, NY)), *pairs,
            dma((2,)), dma((2, 2, NY)), dma((2, 2, NY // 2)), dma((2, NY, 2, 2)), dma((2, 2, 2)),
            dma((2, NX, 2, NZ // 2)), dma((2, width // TILE)),
        ],
        compiler_params=pltpu.CompilerParams(
            collective_id=0, has_side_effects=True, vmem_limit_bytes=44 << 20),
        name="layer",
    )(qkv, grad, w)


def per_device(qkv, grad_out, w_qkv):
    factor = 1.0 / math.sqrt(DH * DH * NY * lax.axis_size("ctx"))
    return layer(qkv[0], grad_out[0], w_qkv, factor)[None]


def solution(mesh):
    spec = P(None, ("ctx", "head"), None)
    return jax.shard_map(
        per_device, mesh=mesh, in_specs=(spec, spec, P("ctx", "head")), out_specs=spec, check_vma=False)
```

```python
import functools
import math

import jax
import jax.numpy as jnp
from jax import lax
from jax.experimental import pallas as pl
from jax.experimental.pallas import tpu as pltpu
from jax.sharding import PartitionSpec as P

DH = 128
W3 = 3 * DH
MESH = pl.DeviceIdType.MESH
NX, NY, NZ = 4, 8, 8
F32, BF16 = jnp.float32, jnp.bfloat16
TILE = 256
ORDER = [
    "m0", "S0", "l0", "m1", "i0", "Z00", "C1", "R1", "L0", "i1", "t0", "Z01", "z0", "L1", "C2", "R2",
    "x0", "Z10", "Z20", "L2", "b0", "t1", "Z02", "R3", "z1", "Z11", "L3", "x1", "Z21", "L4", "b1", "Z30",
    "R4", "i2", "i3", "Z12", "L5", "f0", "Z22", "L6", "Z31", "L7", "f1", "Z32",
]


def where_am_i():
    ctx, y = lax.axis_index("ctx"), lax.axis_index("head")
    c, xz = lax.rem(ctx, 2), lax.div(ctx, 2)
    return lax.div(xz, NZ), y, lax.rem(xz, NZ), c


def device(x, y, z, c):
    return ((x * NZ + z) * 2 + c, y)


def nn(a, b):
    return lax.dot_general(a, b, (((1,), (0,)), ((), ())), preferred_element_type=F32)


def nt(a, b):
    return lax.dot_general(a, b, (((1,), (1,)), ((), ())), preferred_element_type=F32)


def tn(a, b):
    return lax.dot_general(a, b, (((0,), (0,)), ((), ())), preferred_element_type=F32)


def lanes(index, width):
    return pl.ds(pl.multiple_of(index * width, width), width)


def layer_kernel(
    factor, qkv_hbm, grad_hbm, w_hbm, out_ref,
    qkv_ref, grad_ref, w_ref, got_qkv, got_grad, states, arrived, before, intra,
    total, z_in, x_in, z_out, base, grads, weight, give, take,
    load_sem, core_sem, state_sem, z_sem, x_sem, b_sem, p_sem,
    first_sem, got_sem, ring_sem, line_sem, cross_sem, long_sem, tile_sem,
):
    x, y, z, c = where_am_i()
    other = 1 - c
    ring_y = lambda k: device(x, lax.rem(y + k, NY), z, c)
    ring_z = lambda k: device(x, y, lax.rem(z + k, NZ), c)
    ring_x = lambda k: device(lax.rem(x + k, NX), y, z, c)
    partner = device(x, y, z, other)

    loads = [
        pltpu.make_async_copy(w_hbm, w_ref, load_sem.at[0]),
        pltpu.make_async_copy(qkv_hbm, qkv_ref, load_sem.at[1]),
        pltpu.make_async_copy(grad_hbm, grad_ref, load_sem.at[2]),
    ]
    for load in loads:
        load.start()

    barrier = pltpu.get_barrier_semaphore()
    everyone = [partner] + [ring_y(k) for k in range(1, NY)]
    everyone += [ring_z(k) for k in range(1, NZ)] + [ring_x(k) for k in range(1, NX)]
    everyone += [device(x, lax.rem(y + k * other, NY), lax.rem(z + k * c, NZ), other) for k in range(1, NZ)]
    for peer in everyone:
        pl.semaphore_signal(barrier, inc=1, device_id=peer, device_id_type=MESH)
    pl.semaphore_wait(barrier, len(everyone))

    def remote(src, dst, sems, at, peer):
        return pltpu.make_async_remote_copy(
            src, dst, sems.at[(0,) + at], sems.at[(1,) + at], device_id=peer, device_id_type=MESH)

    def y_of(k):
        return lax.rem(y + k, NY)

    def loop(first, last, do):
        def one(k, carry):
            do(k)
            return carry

        lax.fori_loop(first, last, one, 0)

    spot = x * NZ + z
    rows = w_ref.shape[0]
    half = rows // 2
    own_half = pl.ds(pl.multiple_of(c * rows, rows), rows)

    def first_to(core, k):
        peer = device(x, lax.rem(y + k * c, NY), lax.rem(z + k * other, NZ), core)
        return pltpu.make_async_remote_copy(
            w_hbm.at[:, lanes(core, W3)], weight.at[y, spot, own_half],
            first_sem.at[core, k], got_sem.at[c, k], device_id=peer, device_id_type=MESH)

    def first_from(row, k):
        block = weight.at[y, spot, pl.ds(row * rows, rows)]
        return pltpu.make_async_remote_copy(
            block, block, first_sem.at[row, k], got_sem.at[row, k], device_id=partner, device_id_type=MESH)

    first_to(other, 0).start()

    def start_first(k):
        for core in range(2):
            first_to(core, k).start()

    loop(1, NY, start_first)

    def swap(j):
        return remote(qkv_hbm.at[:, lanes(2 * j + other, W3)], got_qkv.at[:, lanes(j, W3)], core_sem, (0, j), partner)

    def swap_grad(j):
        return remote(grad_hbm.at[:, lanes(2 * j + other, DH)], got_grad.at[:, lanes(j, DH)], core_sem, (1, j), partner)

    loop(1, NY + 1, lambda k: swap(y_of(k)).start())
    loop(1, NY + 1, lambda k: swap_grad(y_of(k)).start())

    def side(way, last):
        return pl.ds(0 if way > 0 else half, half) if last else pl.ds(0, rows)

    def side_z(way, last):
        return pl.ds(rows if way > 0 else rows + half, half) if last else pl.ds(rows, rows)

    def way_at(way):
        return 0 if way > 0 else 1

    def same(ref, sems, at, peer):
        return remote(ref, ref, sems, at, peer)

    def a_ring(way, d):
        block = weight.at[lax.rem(y - way * d + NY, NY), pl.ds(x * NZ, NZ), side(way, d == NY // 2 - 1)]
        return same(block, ring_sem, (way_at(way), d), ring_y(way % NY))

    order = [0, -1, 1, -2, 2, -3, 3, 4]

    def a_line(t, way, d):
        at = lax.rem(x - way * d + NX, NX)
        block = weight.at[lax.rem(y + order[t] + NY, NY), pl.ds(at * NZ, NZ), side(way, d == 1)]
        return same(block, line_sem, (t, way_at(way), d), ring_x(way % NX))

    def b_cross(way, d):
        at = lax.rem(x - way * d + NX, NX)
        return same(weight.at[:, at * NZ + z, side_z(way, d == 1)], cross_sem, (way_at(way), d), ring_x(way % NX))

    near = [0, -1, 1, 2]

    def b_long(b, way, d):
        at = lax.rem(x + near[b] + NX, NX) * NZ + lax.rem(z - way * d + NZ, NZ)
        block = weight.at[:, at, side_z(way, d == NZ // 2 - 1)]
        return same(block, long_sem, (b, way_at(way), d), ring_z(way % NZ))

    both = (1, -1)

    def set_off():
        loop(c, NY, lambda k: first_from(1, k).wait_recv())
        for way in both:
            b_cross(way, 0).start()
        for way in both:
            b_long(0, way, 0).start()
        loop(other, NZ, lambda k: first_from(0, k).wait_recv())
        for way in both:
            a_ring(way, 0).start()

    def start_line():
        for way in both:
            a_line(0, way, 0).start()

    def pass_ring(i):
        for n, way in enumerate(both):
            a_ring(way, i - 1).wait_recv()
            if i < NY // 2:
                a_ring(way, i).start()
                for on in both:
                    a_line(2 * i - 1 + n, on, 0).start()
        if i == NY // 2:
            for on in both:
                a_line(NY - 1, on, 0).start()

    def pass_cross(i):
        for way in both:
            b_cross(way, i - 1).wait_recv()
            if i == 1:
                b_cross(way, 1).start()
        for b in ((1, 2), (3,))[i - 1]:
            for way in both:
                b_long(b, way, 0).start()

    def pass_long(b, d):
        for way in both:
            b_long(b, way, d).wait_recv()
            b_long(b, way, d + 1).start()

    def pass_line(t):
        for way in both:
            a_line(t, way, 0).wait_recv()
            a_line(t, way, 1).start()

    loads[0].wait()
    weight[y, spot, own_half, :] = w_ref[:, lanes(c, W3)]

    def own_rows(j):
        at = (2 * j + c) * W3
        part = lambda i: qkv_ref[:, pl.ds(pl.multiple_of(at + i * DH, DH), DH)]
        return part(0), part(1), part(2), grad_ref[:, lanes(2 * j + c, DH)]

    def got_rows(j):
        part = lambda i: got_qkv[:, pl.ds(pl.multiple_of(j * W3 + i * DH, DH), DH)]
        return part(0), part(1), part(2), got_grad[:, lanes(j, DH)]

    sides = ((c, 0, own_rows), (other, 1, got_rows))

    def state_copy(kind, k):
        return remote(states.at[kind, y_of(k)], arrived.at[kind, y], state_sem, (kind, k), ring_y(k))

    def block_states(kind, into, j):
        for slot, _, rows_of in sides:
            q, k, v, g = rows_of(j)
            into[kind, j, slot] = (tn(q, g) if kind else tn(k, v)).astype(BF16)

    def make_states(kind):
        wait = swap_grad if kind else swap

        def one(k):
            wait(y_of(k)).wait()
            block_states(kind, states, y_of(k))
            state_copy(kind, k).start()

        loop(1, NY, one)
        wait(y).wait()
        block_states(kind, arrived, y)

    causal = lax.broadcasted_iota(jnp.int32, (DH, DH), 0) >= lax.broadcasted_iota(jnp.int32, (DH, DH), 1)

    def inside(j):
        for slot, _, rows_of in sides:
            q, k, v, g = rows_of(j)
            gv = jnp.where(causal, nt(g, v), 0.0).astype(BF16)
            qk = jnp.where(causal, nt(q, k), 0.0).astype(BF16)
            intra[slot, j, 0] = nn(gv, k)
            intra[slot, j, 1] = tn(gv, q)
            intra[slot, j, 2] = tn(qk, g)

    part = DH // NZ

    def slice_of(i):
        return pl.ds(pl.multiple_of(i * part, part), part)

    def z_copy(kind, k):
        return remote(total.at[kind, slice_of(lax.rem(z + k, NZ))], z_in.at[kind, z], z_sem, (kind, k), ring_z(k))

    def x_copy(kind, k):
        return remote(x_in.at[kind, x], x_in.at[kind, x], x_sem, (kind, k), ring_x(k))

    def b_copy(kind, k):
        return remote(z_out.at[kind, lax.rem(z + k, NZ)], base.at[kind, slice_of(z)], b_sem, (kind, k), ring_z(k))

    def p_copy(kind, k):
        return remote(states.at[kind, y_of(k)], before.at[kind, y], p_sem, (kind, k), ring_y(k))

    def scan_totals(kind):
        loop(1, NY, lambda k: state_copy(kind, k).wait())
        acc = jnp.zeros((DH, DH), F32)
        for j in range(NY):
            acc = acc + arrived[kind, j, 0].astype(F32) + arrived[kind, j, 1].astype(F32)
        total[kind] = acc
        for k in range(1, NZ):
            z_copy(kind, k).start()
        z_in[kind, z] = total[kind, slice_of(z), :]

    def scan_over_z(kind):
        for k in range(1, NZ):
            z_copy(kind, k).wait()
        acc = z_in[kind, 0]
        for i in range(1, NZ):
            acc = acc + z_in[kind, i]
        x_in[kind, x] = acc
        for k in range(1, NX):
            x_copy(kind, k).start()

    def scan_over_x(kind):
        for k in range(1, NX):
            x_copy(kind, k).wait()
        acc = jnp.zeros((part, DH), F32)
        for i in range(NX):
            acc = acc + jnp.where(i > x if kind else i < x, x_in[kind, i], 0.0)
        for i in reversed(range(NZ)) if kind else range(NZ):
            z_out[kind, i] = acc
            acc = acc + z_in[kind, i]
        for k in range(1, NZ):
            b_copy(kind, k).start()
        base[kind, slice_of(z), :] = z_out[kind, z]

    def scan_blocks(kind):
        for k in range(1, NZ):
            b_copy(kind, k).wait()
        acc = base[kind]
        for slot in (1, 0) if kind else (0, 1):
            for j in reversed(range(NY)) if kind else range(NY):
                states[kind, j, slot] = acc.astype(BF16)
                acc = acc + arrived[kind, j, slot].astype(F32)
        loop(1, NY, lambda k: p_copy(kind, k).start())
        for slot in range(2):
            before[kind, y, slot] = states[kind, y, slot]

    def finish(kind, j):
        for slot, mine, rows_of in sides:
            q, k, v, g = rows_of(j)
            state = before[kind, j, slot]
            at = lambda i: pl.ds(pl.multiple_of(j * W3 + i * DH, DH), DH)
            if kind == 0:
                grads[mine, :, at(0)] = ((intra[slot, j, 0] + nt(g, state)) * factor).astype(BF16)
            else:
                grads[mine, :, at(1)] = ((intra[slot, j, 1] + nt(v, state)) * factor).astype(BF16)
                grads[mine, :, at(2)] = ((intra[slot, j, 2] + nn(k, state)) * factor).astype(BF16)

    def finish_all(kind):
        finish(kind, y)

        def one(k):
            p_copy(kind, k).wait()
            finish(kind, lax.rem(y - k + NY, NY))

        loop(1, NY, one)

    def insides(first, last):
        loop(first, last, inside)

    tiles = NX * NZ * 2 * rows // TILE
    each = tiles // NX
    spots = TILE // (2 * rows)

    def tile_copy(i):
        return remote(give.at[:, lanes(i, TILE)], take.at[:, lanes(i, TILE)], tile_sem, (i,), partner)

    def project(i):
        acc = jnp.zeros((2 * DH, TILE), F32)
        for j in range(NY):
            left = grads[:, :, j * W3:(j + 1) * W3].reshape(2 * DH, W3)
            right = weight[j, pl.ds(i * spots, spots)].reshape(TILE, W3)
            acc = acc + nt(left, right)
        give[:, lanes(i, TILE)] = acc[DH:].astype(BF16)
        tile_copy(i).start()
        out_ref[:, lanes(i, TILE)] = acc[:DH]

    def project_x(b):
        at = lax.rem(x + near[b] + NX, NX) * each
        loop(at, at + each, project)

    def add_partner(i):
        tile_copy(i).wait()
        out_ref[:, lanes(i, TILE)] += take[:, lanes(i, TILE)].astype(F32)

    def load_and_make(kind):
        loads[1 + kind].wait()
        make_states(kind)

    acts = {
        "m": load_and_make, "t": scan_totals, "z": scan_over_z, "x": scan_over_x, "b": scan_blocks, "f": finish_all,
        "i": lambda n: insides(2 * n, 2 * n + 2), "S": lambda n: set_off(), "R": pass_ring, "C": pass_cross,
        "L": pass_line, "l": lambda n: start_line(), "Z": lambda n: pass_long(n // 10, n % 10),
    }
    for step in ORDER:
        acts[step[0]](int(step[1:]))

    last = NZ // 2 - 1
    for way in both:
        b_long(0, way, last).wait_recv()
    project_x(0)
    for b in (1, 2):
        for way in both:
            b_long(b, way, last).wait_recv()
        project_x(b)
    for way in both:
        b_long(3, way, last).wait_recv()
        for t in range(NY):
            a_line(t, way, 1).wait_recv()
    project_x(3)
    loop(0, tiles, add_partner)
    first_to(other, 0).wait_send()

    def wait_first(k):
        for core in range(2):
            first_to(core, k).wait_send()

    loop(1, NY, wait_first)
    for way in both:
        for d in range(2):
            b_cross(way, d).wait_send()
            for t in range(NY):
                a_line(t, way, d).wait_send()
        for d in range(NY // 2):
            a_ring(way, d).wait_send()
        for b in range(NX):
            for d in range(NZ // 2):
                b_long(b, way, d).wait_send()


def layer(qkv, grad, w, factor):
    part = DH // NZ
    rows = w.shape[0]
    width = NX * NZ * 2 * rows
    dma = pltpu.SemaphoreType.DMA
    state = pltpu.VMEM((2, NY, 2, DH, DH), BF16)
    return pl.pallas_call(
        functools.partial(layer_kernel, factor),
        out_shape=jax.ShapeDtypeStruct((DH, width), F32),
        in_specs=[pl.BlockSpec(memory_space=pltpu.HBM)] * 3,
        out_specs=pl.BlockSpec(memory_space=pltpu.VMEM),
        scratch_shapes=[
            pltpu.VMEM(qkv.shape, BF16), pltpu.VMEM(grad.shape, BF16), pltpu.VMEM(w.shape, BF16),
            pltpu.VMEM((DH, NY * W3), BF16), pltpu.VMEM((DH, NY * DH), BF16),
            state, state, state,
            pltpu.VMEM((2, NY, 3, DH, DH), F32),
            pltpu.VMEM((2, DH, DH), F32), pltpu.VMEM((2, NZ, part, DH), F32),
            pltpu.VMEM((2, NX, part, DH), F32), pltpu.VMEM((2, NZ, part, DH), F32),
            pltpu.VMEM((2, DH, DH), F32),
            pltpu.VMEM((2, DH, NY * W3), BF16),
            pltpu.VMEM((NY, NX * NZ, 2 * rows, W3), BF16),
            pltpu.VMEM((DH, width), BF16), pltpu.VMEM((DH, width), BF16),
            dma((3,)), dma((2, 2, NY)), dma((2, 2, NY)), dma((2, 2, NZ)), dma((2, 2, NX)),
            dma((2, 2, NZ)), dma((2, 2, NY)),
            dma((2, NY)), dma((2, NY)), dma((2, 2, NY // 2)), dma((2, NY, 2, 2)), dma((2, 2, 2)),
            dma((2, NX, 2, NZ // 2)), dma((2, width // TILE)),
        ],
        compiler_params=pltpu.CompilerParams(
            collective_id=0, has_side_effects=True, vmem_limit_bytes=60 << 20),
        name="layer",
    )(qkv, grad, w)


def per_device(qkv, grad_out, w_qkv):
    factor = 1.0 / math.sqrt(DH * DH * NY * lax.axis_size("ctx"))
    return layer(qkv[0], grad_out[0], w_qkv, factor)[None]


def solution(mesh):
    spec = P(None, ("ctx", "head"), None)
    return jax.shard_map(
        per_device, mesh=mesh, in_specs=(spec, spec, P("ctx", "head")), out_specs=spec, check_vma=False)
```

```python
import functools
import math

import jax
import jax.numpy as jnp
from jax import lax
from jax.experimental import pallas as pl
from jax.experimental.pallas import tpu as pltpu
from jax.sharding import PartitionSpec as P

DH = 128
W3 = 3 * DH
MESH = pl.DeviceIdType.MESH
NX, NY, NZ = 4, 8, 8
F32, BF16 = jnp.float32, jnp.bfloat16
TILE = 256
ORDER = [
    "m0", "S0", "l0", "m1", "Z00", "C1", "R1", "L0", "i0", "i1", "t0", "Z01", "z0", "L1", "C2", "R2",
    "x0", "Z10", "Z20", "L2", "b0", "t1", "Z02", "R3", "z1", "Z11", "L3", "x1", "Z21", "L4", "b1", "Z30",
    "R4", "i2", "i3", "Z12", "L5", "f0", "Z22", "L6", "Z31", "L7", "f1", "Z32",
]


def where_am_i():
    ctx, y = lax.axis_index("ctx"), lax.axis_index("head")
    c, xz = lax.rem(ctx, 2), lax.div(ctx, 2)
    return lax.div(xz, NZ), y, lax.rem(xz, NZ), c


def device(x, y, z, c):
    return ((x * NZ + z) * 2 + c, y)


def nn(a, b):
    return lax.dot_general(a, b, (((1,), (0,)), ((), ())), preferred_element_type=F32)


def nt(a, b):
    return lax.dot_general(a, b, (((1,), (1,)), ((), ())), preferred_element_type=F32)


def tn(a, b):
    return lax.dot_general(a, b, (((0,), (0,)), ((), ())), preferred_element_type=F32)


def lanes(index, width):
    return pl.ds(pl.multiple_of(index * width, width), width)


def layer_kernel(
    factor, qkv_hbm, grad_hbm, w_hbm, out_ref,
    qkv_ref, grad_ref, w_ref, got_qkv, got_grad, states, arrived, before, intra,
    total, z_in, x_in, z_out, base, grads, weight, give, take,
    load_sem, core_sem, state_sem, z_sem, x_sem, b_sem, p_sem,
    first_sem, got_sem, ring_sem, line_sem, cross_sem, long_sem, tile_sem,
):
    x, y, z, c = where_am_i()
    other = 1 - c
    ring_y = lambda k: device(x, lax.rem(y + k, NY), z, c)
    ring_z = lambda k: device(x, y, lax.rem(z + k, NZ), c)
    ring_x = lambda k: device(lax.rem(x + k, NX), y, z, c)
    partner = device(x, y, z, other)

    loads = [
        pltpu.make_async_copy(w_hbm, w_ref, load_sem.at[0]),
        pltpu.make_async_copy(qkv_hbm, qkv_ref, load_sem.at[1]),
        pltpu.make_async_copy(grad_hbm, grad_ref, load_sem.at[2]),
    ]
    for load in loads:
        load.start()

    barrier = pltpu.get_barrier_semaphore()
    everyone = [partner] + [ring_y(k) for k in range(1, NY)]
    everyone += [ring_z(k) for k in range(1, NZ)] + [ring_x(k) for k in range(1, NX)]
    everyone += [device(x, lax.rem(y + k * other, NY), lax.rem(z + k * c, NZ), other) for k in range(1, NZ)]
    for peer in everyone:
        pl.semaphore_signal(barrier, inc=1, device_id=peer, device_id_type=MESH)
    pl.semaphore_wait(barrier, len(everyone))

    def remote(src, dst, sems, at, peer):
        return pltpu.make_async_remote_copy(
            src, dst, sems.at[(0,) + at], sems.at[(1,) + at], device_id=peer, device_id_type=MESH)

    def y_of(k):
        return lax.rem(y + k, NY)

    def loop(first, last, do):
        def one(k, carry):
            do(k)
            return carry

        lax.fori_loop(first, last, one, 0)

    spot = x * NZ + z
    rows = w_ref.shape[0]
    half = rows // 2
    own_half = pl.ds(pl.multiple_of(c * rows, rows), rows)

    def first_to(core, k):
        peer = device(x, lax.rem(y + k * c, NY), lax.rem(z + k * other, NZ), core)
        return pltpu.make_async_remote_copy(
            w_hbm.at[:, lanes(core, W3)], weight.at[y, spot, own_half],
            first_sem.at[core, k], got_sem.at[c, k], device_id=peer, device_id_type=MESH)

    def first_from(row, k):
        block = weight.at[y, spot, pl.ds(row * rows, rows)]
        return pltpu.make_async_remote_copy(
            block, block, first_sem.at[row, k], got_sem.at[row, k], device_id=partner, device_id_type=MESH)

    first_to(other, 0).start()

    def start_first(k):
        for core in range(2):
            first_to(core, k).start()

    loop(1, NY, start_first)

    def swap(j):
        return remote(qkv_hbm.at[:, lanes(2 * j + other, W3)], got_qkv.at[:, lanes(j, W3)], core_sem, (0, j), partner)

    def swap_grad(j):
        return remote(grad_hbm.at[:, lanes(2 * j + other, DH)], got_grad.at[:, lanes(j, DH)], core_sem, (1, j), partner)

    loop(1, NY + 1, lambda k: swap(y_of(k)).start())
    loop(1, NY + 1, lambda k: swap_grad(y_of(k)).start())

    def side(way, last):
        return pl.ds(0 if way > 0 else half, half) if last else pl.ds(0, rows)

    def side_z(way, last):
        return pl.ds(rows if way > 0 else rows + half, half) if last else pl.ds(rows, rows)

    def way_at(way):
        return 0 if way > 0 else 1

    def same(ref, sems, at, peer):
        return remote(ref, ref, sems, at, peer)

    def a_ring(way, d):
        block = weight.at[lax.rem(y - way * d + NY, NY), pl.ds(x * NZ, NZ), side(way, d == NY // 2 - 1)]
        return same(block, ring_sem, (way_at(way), d), ring_y(way % NY))

    order = [0, -1, 1, -2, 2, -3, 3, 4]

    def a_line(t, way, d):
        at = lax.rem(x - way * d + NX, NX)
        block = weight.at[lax.rem(y + order[t] + NY, NY), pl.ds(at * NZ, NZ), side(way, d == 1)]
        return same(block, line_sem, (t, way_at(way), d), ring_x(way % NX))

    def b_cross(way, d):
        at = lax.rem(x - way * d + NX, NX)
        return same(weight.at[:, at * NZ + z, side_z(way, d == 1)], cross_sem, (way_at(way), d), ring_x(way % NX))

    near = [0, -1, 1, 2]

    def b_long(b, way, d):
        at = lax.rem(x + near[b] + NX, NX) * NZ + lax.rem(z - way * d + NZ, NZ)
        block = weight.at[:, at, side_z(way, d == NZ // 2 - 1)]
        return same(block, long_sem, (b, way_at(way), d), ring_z(way % NZ))

    both = (1, -1)

    def set_off():
        loop(c, NY, lambda k: first_from(1, k).wait_recv())
        for way in both:
            b_cross(way, 0).start()
        for way in both:
            b_long(0, way, 0).start()
        loop(other, NZ, lambda k: first_from(0, k).wait_recv())
        for way in both:
            a_ring(way, 0).start()

    def start_line():
        for way in both:
            a_line(0, way, 0).start()

    def pass_ring(i):
        for n, way in enumerate(both):
            a_ring(way, i - 1).wait_recv()
            if i < NY // 2:
                a_ring(way, i).start()
                for on in both:
                    a_line(2 * i - 1 + n, on, 0).start()
        if i == NY // 2:
            for on in both:
                a_line(NY - 1, on, 0).start()

    def pass_cross(i):
        for way in both:
            b_cross(way, i - 1).wait_recv()
            if i == 1:
                b_cross(way, 1).start()
        for b in ((1, 2), (3,))[i - 1]:
            for way in both:
                b_long(b, way, 0).start()

    def pass_long(b, d):
        for way in both:
            b_long(b, way, d).wait_recv()
            b_long(b, way, d + 1).start()

    def pass_line(t):
        for way in both:
            a_line(t, way, 0).wait_recv()
            a_line(t, way, 1).start()

    loads[0].wait()
    weight[y, spot, own_half, :] = w_ref[:, lanes(c, W3)]

    def own_rows(j):
        at = (2 * j + c) * W3
        part = lambda i: qkv_ref[:, pl.ds(pl.multiple_of(at + i * DH, DH), DH)]
        return part(0), part(1), part(2), grad_ref[:, lanes(2 * j + c, DH)]

    def got_rows(j):
        part = lambda i: got_qkv[:, pl.ds(pl.multiple_of(j * W3 + i * DH, DH), DH)]
        return part(0), part(1), part(2), got_grad[:, lanes(j, DH)]

    sides = ((c, 0, own_rows), (other, 1, got_rows))

    def state_copy(kind, k):
        return remote(states.at[kind, y_of(k)], arrived.at[kind, y], state_sem, (kind, k), ring_y(k))

    def block_states(kind, into, j):
        for slot, _, rows_of in sides:
            q, k, v, g = rows_of(j)
            into[kind, j, slot] = (tn(q, g) if kind else tn(k, v)).astype(BF16)

    def make_states(kind):
        wait = swap_grad if kind else swap

        def one(k):
            wait(y_of(k)).wait()
            block_states(kind, states, y_of(k))
            state_copy(kind, k).start()

        loop(1, NY, one)
        wait(y).wait()
        block_states(kind, arrived, y)

    causal = lax.broadcasted_iota(jnp.int32, (DH, DH), 0) >= lax.broadcasted_iota(jnp.int32, (DH, DH), 1)

    def inside(j):
        for slot, _, rows_of in sides:
            q, k, v, g = rows_of(j)
            gv = jnp.where(causal, nt(g, v), 0.0).astype(BF16)
            qk = jnp.where(causal, nt(q, k), 0.0).astype(BF16)
            intra[slot, j, 0] = nn(gv, k)
            intra[slot, j, 1] = tn(gv, q)
            intra[slot, j, 2] = tn(qk, g)

    part = DH // NZ

    def slice_of(i):
        return pl.ds(pl.multiple_of(i * part, part), part)

    def z_copy(kind, k):
        return remote(total.at[kind, slice_of(lax.rem(z + k, NZ))], z_in.at[kind, z], z_sem, (kind, k), ring_z(k))

    def x_copy(kind, k):
        return remote(x_in.at[kind, x], x_in.at[kind, x], x_sem, (kind, k), ring_x(k))

    def b_copy(kind, k):
        return remote(z_out.at[kind, lax.rem(z + k, NZ)], base.at[kind, slice_of(z)], b_sem, (kind, k), ring_z(k))

    def p_copy(kind, k):
        return remote(states.at[kind, y_of(k)], before.at[kind, y], p_sem, (kind, k), ring_y(k))

    def scan_totals(kind):
        loop(1, NY, lambda k: state_copy(kind, k).wait())
        acc = jnp.zeros((DH, DH), F32)
        for j in range(NY):
            acc = acc + arrived[kind, j, 0].astype(F32) + arrived[kind, j, 1].astype(F32)
        total[kind] = acc
        for k in range(1, NZ):
            z_copy(kind, k).start()
        z_in[kind, z] = total[kind, slice_of(z), :]

    def scan_over_z(kind):
        for k in range(1, NZ):
            z_copy(kind, k).wait()
        acc = z_in[kind, 0]
        for i in range(1, NZ):
            acc = acc + z_in[kind, i]
        x_in[kind, x] = acc
        for k in range(1, NX):
            x_copy(kind, k).start()

    def scan_over_x(kind):
        for k in range(1, NX):
            x_copy(kind, k).wait()
        acc = jnp.zeros((part, DH), F32)
        for i in range(NX):
            acc = acc + jnp.where(i > x if kind else i < x, x_in[kind, i], 0.0)
        for i in reversed(range(NZ)) if kind else range(NZ):
            z_out[kind, i] = acc
            acc = acc + z_in[kind, i]
        for k in range(1, NZ):
            b_copy(kind, k).start()
        base[kind, slice_of(z), :] = z_out[kind, z]

    def scan_blocks(kind):
        for k in range(1, NZ):
            b_copy(kind, k).wait()
        acc = base[kind]
        for slot in (1, 0) if kind else (0, 1):
            for j in reversed(range(NY)) if kind else range(NY):
                states[kind, j, slot] = acc.astype(BF16)
                acc = acc + arrived[kind, j, slot].astype(F32)
        loop(1, NY, lambda k: p_copy(kind, k).start())
        for slot in range(2):
            before[kind, y, slot] = states[kind, y, slot]

    def finish(kind, j):
        for slot, mine, rows_of in sides:
            q, k, v, g = rows_of(j)
            state = before[kind, j, slot]
            at = lambda i: pl.ds(pl.multiple_of(j * W3 + i * DH, DH), DH)
            if kind == 0:
                grads[mine, :, at(0)] = ((intra[slot, j, 0] + nt(g, state)) * factor).astype(BF16)
            else:
                grads[mine, :, at(1)] = ((intra[slot, j, 1] + nt(v, state)) * factor).astype(BF16)
                grads[mine, :, at(2)] = ((intra[slot, j, 2] + nn(k, state)) * factor).astype(BF16)

    def finish_all(kind):
        finish(kind, y)

        def one(k):
            p_copy(kind, k).wait()
            finish(kind, lax.rem(y - k + NY, NY))

        loop(1, NY, one)

    def insides(first, last):
        loop(first, last, inside)

    tiles = NX * NZ * 2 * rows // TILE
    each = tiles // NX
    spots = TILE // (2 * rows)

    def tile_copy(i):
        return remote(give.at[:, lanes(i, TILE)], take.at[:, lanes(i, TILE)], tile_sem, (i,), partner)

    def project(i):
        acc = jnp.zeros((2 * DH, TILE), F32)
        for j in range(NY):
            left = grads[:, :, j * W3:(j + 1) * W3].reshape(2 * DH, W3)
            right = weight[j, pl.ds(i * spots, spots)].reshape(TILE, W3)
            acc = acc + nt(left, right)
        give[:, lanes(i, TILE)] = acc[DH:].astype(BF16)
        tile_copy(i).start()
        out_ref[:, lanes(i, TILE)] = acc[:DH]

    def project_x(b):
        at = lax.rem(x + near[b] + NX, NX) * each
        loop(at, at + each, project)

    def add_partner(i):
        tile_copy(i).wait()
        out_ref[:, lanes(i, TILE)] += take[:, lanes(i, TILE)].astype(F32)

    def load_and_make(kind):
        loads[1 + kind].wait()
        make_states(kind)

    acts = {
        "m": load_and_make, "t": scan_totals, "z": scan_over_z, "x": scan_over_x, "b": scan_blocks, "f": finish_all,
        "i": lambda n: insides(2 * n, 2 * n + 2), "S": lambda n: set_off(), "R": pass_ring, "C": pass_cross,
        "L": pass_line, "l": lambda n: start_line(), "Z": lambda n: pass_long(n // 10, n % 10),
    }
    for step in ORDER:
        acts[step[0]](int(step[1:]))

    last = NZ // 2 - 1
    for way in both:
        b_long(0, way, last).wait_recv()
    project_x(0)
    for b in (1, 2):
        for way in both:
            b_long(b, way, last).wait_recv()
        project_x(b)
    for way in both:
        b_long(3, way, last).wait_recv()
        for t in range(NY):
            a_line(t, way, 1).wait_recv()
    project_x(3)
    loop(0, tiles, add_partner)
    first_to(other, 0).wait_send()

    def wait_first(k):
        for core in range(2):
            first_to(core, k).wait_send()

    loop(1, NY, wait_first)
    for way in both:
        for d in range(2):
            b_cross(way, d).wait_send()
            for t in range(NY):
                a_line(t, way, d).wait_send()
        for d in range(NY // 2):
            a_ring(way, d).wait_send()
        for b in range(NX):
            for d in range(NZ // 2):
                b_long(b, way, d).wait_send()


def layer(qkv, grad, w, factor):
    part = DH // NZ
    rows = w.shape[0]
    width = NX * NZ * 2 * rows
    dma = pltpu.SemaphoreType.DMA
    state = pltpu.VMEM((2, NY, 2, DH, DH), BF16)
    return pl.pallas_call(
        functools.partial(layer_kernel, factor),
        out_shape=jax.ShapeDtypeStruct((DH, width), F32),
        in_specs=[pl.BlockSpec(memory_space=pltpu.HBM)] * 3,
        out_specs=pl.BlockSpec(memory_space=pltpu.VMEM),
        scratch_shapes=[
            pltpu.VMEM(qkv.shape, BF16), pltpu.VMEM(grad.shape, BF16), pltpu.VMEM(w.shape, BF16),
            pltpu.VMEM((DH, NY * W3), BF16), pltpu.VMEM((DH, NY * DH), BF16),
            state, state, state,
            pltpu.VMEM((2, NY, 3, DH, DH), F32),
            pltpu.VMEM((2, DH, DH), F32), pltpu.VMEM((2, NZ, part, DH), F32),
            pltpu.VMEM((2, NX, part, DH), F32), pltpu.VMEM((2, NZ, part, DH), F32),
            pltpu.VMEM((2, DH, DH), F32),
            pltpu.VMEM((2, DH, NY * W3), BF16),
            pltpu.VMEM((NY, NX * NZ, 2 * rows, W3), BF16),
            pltpu.VMEM((DH, width), BF16), pltpu.VMEM((DH, width), BF16),
            dma((3,)), dma((2, 2, NY)), dma((2, 2, NY)), dma((2, 2, NZ)), dma((2, 2, NX)),
            dma((2, 2, NZ)), dma((2, 2, NY)),
            dma((2, NY)), dma((2, NY)), dma((2, 2, NY // 2)), dma((2, NY, 2, 2)), dma((2, 2, 2)),
            dma((2, NX, 2, NZ // 2)), dma((2, width // TILE)),
        ],
        compiler_params=pltpu.CompilerParams(
            collective_id=0, has_side_effects=True, vmem_limit_bytes=60 << 20),
        name="layer",
    )(qkv, grad, w)


def per_device(qkv, grad_out, w_qkv):
    factor = 1.0 / math.sqrt(DH * DH * NY * lax.axis_size("ctx"))
    return layer(qkv[0], grad_out[0], w_qkv, factor)[None]


def solution(mesh):
    spec = P(None, ("ctx", "head"), None)
    return jax.shard_map(
        per_device, mesh=mesh, in_specs=(spec, spec, P("ctx", "head")), out_specs=spec, check_vma=False)
```
